32 devices in a mesh: expert: 16 (over z, x, core), shard: 2 (over y).
Axes of the slice: x: 2, y: 2, z: 4, core: 2. Of those that a mesh axis runs over, the one named last changes fastest.
Arguments:
- hidden_in: bfloat16 [4096, 1024], P(('expert', 'shard')), may hold values from -6 to 6
- norm_attn: bfloat16 [1024], P('shard'), may hold values from 0.5 to 1.5
- w_query: bfloat16 [1024, 1024], P('shard'), may hold values from -0.75 to 0.75
- w_key: bfloat16 [1024, 512], P('shard'), may hold values from -0.75 to 0.75
- w_value: bfloat16 [1024, 512], P('shard'), may hold values from -0.1875 to 0.1875
- w_out: bfloat16 [1024, 1024], P('shard'), may hold values from -2.5 to 2.5
- norm_ffn: bfloat16 [1024], P('shard'), may hold values from 0.5 to 1.5
- w_router: bfloat16 [1024, 16], P('shard'), may hold values from -0.09375 to 0.09375
- w_gate_up: bfloat16 [16, 1024, 1024], P('expert'), may hold values from -0.1875 to 0.1875
- w_down: bfloat16 [16, 512, 1024], P('expert'), may hold values from -3 to 3
- routes: int32 [4096, 8], P(('expert', 'shard')), may hold values from 0 to 15, all different within a row; in each aligned block of 128 rows (0 to 127, 128 to 255, ...) at most 80 rows name the same one
- out_grad: bfloat16 [4096, 1024], P(('expert', 'shard')), may hold values from -6 to 6
Outputs:
- output: bfloat16 [4096, 1024], P(('expert', 'shard'))
- input_grad: bfloat16 [4096, 1024], P(('expert', 'shard'))
- norm_attn_grad: float32 [1024], P('shard')
- query_wgrad: float32 [1024, 1024], P('shard')
- key_wgrad: float32 [1024, 512], P('shard')
- value_wgrad: float32 [1024, 512], P('shard')
- out_wgrad: float32 [1024, 1024], P('shard')
- norm_ffn_grad: float32 [1024], P('shard')
- router_wgrad: float32 [1024, 16], P('shard')
- gate_up_wgrad: float32 [16, 1024, 1024], P('expert', None, 'shard')
- down_wgrad: float32 [16, 512, 1024], P('expert', None, 'shard')
The draws below stay inside these ranges and needn't reach their ends.
Inputs may be any that keep to these rules, and one draw needn't show every extreme that they name: `routes`: among the 128 rows of one device (aligned blocks), no expert is named by more than 80 rows, and in some block one expert is named by exactly 80; a row names 8 different experts.
All inputs are finite; a program needn't handle non-finite values.
Results may differ from the reference program's by a relative error of at most 0.02.
Values may be sent and summed in bfloat16 or wider, within the bound.
A program may use at most 128 MiB of HBM per device.

```python
import math
import jax
import jax.numpy as jnp
import numpy as np
from jax import lax

D = 1024
Q_HEADS = 16
KV_HEADS = 8
HEAD_DIM = 64
FF = 512
TOP = 8
TOK_DEV = 128
EXPERTS = 16
TOKENS = 4096
CAP = 80


def steps_of(key, shape, split, smallest, largest):
    gain = 1.0
    for axis_at, parts in split:
        steps = jax.random.uniform(jax.random.fold_in(jax.random.fold_in(key, 6), axis_at), (parts,), jnp.float32, smallest / len(split), largest / len(split))
        gain = gain * jnp.repeat(jnp.exp(steps), shape[axis_at] // parts).reshape((-1,) + (1,) * (len(shape) - 1 - axis_at))
    return gain


def assign_block(stream_key, own, number, rows, count, top, most, slope):
    sequence = jax.random.permutation(stream_key, count)
    crowded, ordinary = shares(count, rows * top, most, slope, True), shares(count, rows * top, most, slope, False)
    places = jnp.arange(count)

    def named(lengths, offset_by):
        used = int((lengths > 0).sum())
        fixed = max(1, used // 4)
        passed = fixed + (places - fixed + offset_by * (used - fixed)) % max(1, count - fixed)
        return jnp.zeros((count,), jnp.int32).at[sequence[jnp.where(places < fixed, places, passed)]].set(jnp.asarray(lengths, jnp.int32))

    lengths = jnp.where(number % 4 == 0, named(crowded, number // 4), named(ordinary, number - number // 4 - 1))
    mixed = jax.random.permutation(jax.random.fold_in(own, 3), count)
    donor, sink = mixed[0:count // 2 * 2:2], mixed[1:count // 2 * 2:2]
    margin = jnp.minimum(lengths[donor] - 1, most - lengths[sink]) // 2
    margin = jnp.where((donor == sequence[0]) | (sink == sequence[0]) | (lengths[sink] == 0), 0, jnp.maximum(margin, 0))
    passed = jax.random.randint(jax.random.fold_in(own, 4), (count // 2,), 0, 1 << 20) % (margin + 1)
    lengths = lengths.at[donor].add(-passed).at[sink].add(passed)
    labels = jnp.searchsorted(jnp.cumsum(lengths), jnp.arange(rows * top), side="right").astype(jnp.int32)
    table = labels.reshape(top, rows).T
    table = table[jax.random.permutation(jax.random.fold_in(own, 1), rows)]
    offset_by = jax.random.randint(jax.random.fold_in(own, 2), (rows, 1), 0, top)
    return jnp.take_along_axis(table, (jnp.arange(top)[None, :] + offset_by) % top, axis=1)


def shares(number_of, total, reach, slope, full):
    portions = [(1 << 20) // math.isqrt(standing ** slope) + 1 for standing in range(1, number_of + 1)]
    largest = reach if full else min(reach, max(-(-total // number_of), total * portions[0] // sum(portions)))
    least = 1 if total - largest >= number_of - 1 else 0
    counts, rest = [largest] + [least] * (number_of - 1), total - largest - least * (number_of - 1)
    while rest > 0:
        candidates = [i for i in range(1, number_of) if counts[i] < largest] or [i for i in range(1, number_of) if counts[i] < reach]
        whole, remaining = sum([portions[i] for i in candidates]), rest
        for i in candidates:
            extra = min(reach - counts[i], max(1, remaining * portions[i] // whole), rest)
            counts[i] = counts[i] + extra
            rest = rest - extra
    return np.array(counts)


def gaussian(stream_key, extent, width, most, split=(), kind=jnp.bfloat16):
    gain = steps_of(stream_key, extent, split, -0.22, 0.18) if split else 1.0
    values = jax.random.normal(stream_key, extent, jnp.float32) * width * gain
    return jnp.minimum(jnp.maximum(values, -most), most).astype(kind)


def setup_inputs(seed: int = 0) -> dict:
    key_list = jax.random.split(jax.random.key(seed), 13)
    hidden_in = gaussian(key_list[0], (TOKENS, D), 1.0, 6.0, ((0, 32),))
    norm_attn = jnp.clip(1.0 + 0.1 * jax.random.normal(key_list[1], (D,), jnp.float32), 0.5, 1.5).astype(jnp.bfloat16)
    w_query = gaussian(key_list[2], (D, Q_HEADS * HEAD_DIM), 0.125, 0.75, ((0, 2),))
    w_key = gaussian(key_list[3], (D, KV_HEADS * HEAD_DIM), 0.125, 0.75, ((0, 2),))
    w_value = gaussian(key_list[4], (D, KV_HEADS * HEAD_DIM), D ** -0.5, 0.1875, ((0, 2),))
    w_out = gaussian(key_list[5], (Q_HEADS * HEAD_DIM, D), 0.4, 2.5, ((0, 2),))
    norm_ffn = jnp.clip(1.0 + 0.1 * jax.random.normal(key_list[6], (D,), jnp.float32), 0.5, 1.5).astype(jnp.bfloat16)
    w_router = gaussian(key_list[7], (D, EXPERTS), 0.015625, 0.09375, ((0, 2),))
    w_gate_up = gaussian(key_list[8], (EXPERTS, D, 2 * FF), D ** -0.5, 0.1875, ((0, 16),))
    w_down = gaussian(key_list[9], (EXPERTS, FF, D), 0.5, 3.0, ((0, 16),))
    routes_keys = jax.random.split(jax.random.fold_in(key_list[10], 1), TOKENS // TOK_DEV)
    routes_turns = jax.random.permutation(jax.random.fold_in(key_list[10], 3), TOKENS // TOK_DEV)
    routes = jax.vmap(lambda own, number: assign_block(jax.random.fold_in(key_list[10], 2), own, number, TOK_DEV, EXPERTS, TOP, CAP, 2))(routes_keys, routes_turns).reshape((TOKENS, TOP))
    out_grad = gaussian(key_list[11], (TOKENS, D), 1.0, 6.0, ((0, 32),))
    return dict(hidden_in=hidden_in, norm_attn=norm_attn, w_query=w_query, w_key=w_key, w_value=w_value, w_out=w_out, norm_ffn=norm_ffn, w_router=w_router, w_gate_up=w_gate_up, w_down=w_down, routes=routes, out_grad=out_grad)


EPSILON = 1e-06
RESIDUAL = 0.22
SCORE_SCALE = 0.015625
NEGATIVE = -1e+30

@jax.custom_vjp
def low(v):
    return lax.optimization_barrier(v.astype(jnp.bfloat16)).astype(jnp.float32)

@jax.custom_vjp
def low_back(v):
    return v

def low_keep(v):
    return (low(v), None)

def low_pass(kept, grad):
    return (grad,)

def back_keep(v):
    return (v, None)

def back_low(kept, grad):
    return (low(grad),)
low.defvjp(low_keep, low_pass)
low_back.defvjp(back_keep, back_low)

def rms_scale(values):
    return lax.rsqrt(lax.optimization_barrier(jnp.mean(values * values, axis=-1, keepdims=True)) + EPSILON)

def normed(values, gain_vec):
    return values * rms_scale(values) * gain_vec

def rotary_tables(length, head_width):
    half_width = head_width // 2
    frequency = 10000.0 ** (-2.0 * jnp.arange(half_width, dtype=jnp.float32) / head_width)
    angles = jnp.arange(length, dtype=jnp.float32)[:, None] * frequency[None, :]
    return (jnp.cos(angles), jnp.sin(angles))

def rotate(values, cosine, sine_table):
    half_width = values.shape[-1] // 2
    first_half = values[..., :half_width]
    second_half = values[..., half_width:]
    cos_b = cosine[:, None, :]
    sin_b = sine_table[:, None, :]
    return jnp.concatenate([first_half * cos_b - second_half * sin_b, second_half * cos_b + first_half * sin_b], axis=-1)

def attention_probs(scores):
    length = scores.shape[-1]
    causal = jnp.arange(length)[:, None] >= jnp.arange(length)[None, :]
    return jax.nn.softmax(jnp.where(causal, scores, NEGATIVE), axis=-1)

def swiglu(gate_up):
    half_width = gate_up.shape[-1] // 2
    return jax.nn.silu(gate_up[..., :half_width]) * gate_up[..., half_width:]

def widen(matrix):
    return matrix.astype(jnp.float32)

def layer(hidden, norm_attn, w_query, w_key, w_value, w_out, norm_ffn, w_router, w_gate_up, w_down, routes):
    blocks = TOKENS // TOK_DEV
    per_step = math.gcd(blocks, max(1, 4096 // TOK_DEV))
    steps_count = blocks // per_step
    step_tokens = per_step * TOK_DEV
    step_slots = per_step * CAP
    row_count = step_tokens * TOP
    groups = Q_HEADS // KV_HEADS
    highest = lax.Precision.HIGHEST
    cosine, sine_table = rotary_tables(TOK_DEV, HEAD_DIM)

    def one_step(inputs):
        tokens_in, routes_in = inputs
        xn_one = low(normed(tokens_in, norm_attn))
        raw_query = low_back(jnp.dot(xn_one, w_query, precision=highest, preferred_element_type=jnp.float32))
        raw_key = low_back(jnp.dot(xn_one, w_key, precision=highest, preferred_element_type=jnp.float32))
        raw_value = low_back(jnp.dot(xn_one, w_value, precision=highest, preferred_element_type=jnp.float32))
        query_low = low(rotate(raw_query.reshape(per_step, TOK_DEV, Q_HEADS, HEAD_DIM), cosine, sine_table))
        query_low = query_low.reshape(per_step, TOK_DEV, KV_HEADS, groups, HEAD_DIM)
        key_low = low(rotate(raw_key.reshape(per_step, TOK_DEV, KV_HEADS, HEAD_DIM), cosine, sine_table))
        value_low = low(raw_value).reshape(per_step, TOK_DEV, KV_HEADS, HEAD_DIM)
        scores = low_back(SCORE_SCALE * jnp.einsum('btkgd,bskd->bkgts', query_low, key_low, precision=highest))
        weights_low = low(attention_probs(scores))
        attended = jnp.einsum('bkgts,bskd->btkgd', weights_low, value_low, precision=highest)
        attended = low(low_back(attended.reshape(step_tokens, Q_HEADS * HEAD_DIM)))
        branch = low_back(jnp.dot(attended, w_out, precision=highest, preferred_element_type=jnp.float32))
        middle = tokens_in + RESIDUAL * branch
        xn_two = low(normed(middle, norm_ffn))
        logits = low_back(jnp.dot(xn_two, w_router, precision=highest, preferred_element_type=jnp.float32))
        gate_values = jax.nn.softmax(jnp.take_along_axis(logits, routes_in, axis=1), axis=-1)
        flat_routes = routes_in.reshape(-1)
        onehot_table = (flat_routes[:, None] == jnp.arange(EXPERTS, dtype=jnp.int32)[None, :]).astype(jnp.int32)
        row_ranks = lax.optimization_barrier(jnp.sum((jnp.cumsum(onehot_table, axis=0) - 1) * onehot_table, axis=1)).astype(jnp.int32)
        slot_index = (flat_routes * step_slots + row_ranks).astype(jnp.int32)
        slot_rows = jnp.full((EXPERTS * step_slots,), row_count, jnp.int32).at[slot_index].set(jnp.arange(row_count, dtype=jnp.int32))
        padded = jnp.concatenate([xn_two, jnp.zeros((1, D), jnp.float32)], axis=0)
        expert_rows = low_back(padded[slot_rows // TOP]).reshape(EXPERTS, step_slots, D)
        gate_up = low_back(jnp.einsum('erd,edf->erf', expert_rows, w_gate_up, precision=highest))
        hidden_low = low(swiglu(gate_up))
        expert_out = low(low_back(jnp.einsum('erf,efd->erd', hidden_low, w_down, precision=highest)))
        chosen_out = expert_out.reshape(EXPERTS * step_slots, D)[slot_index].reshape(step_tokens, TOP, D)
        mixture = lax.optimization_barrier(jnp.sum(gate_values[:, :, None] * chosen_out, axis=1))
        return middle + RESIDUAL * mixture
    tokens_steps = hidden.reshape(steps_count, step_tokens, D)
    routes_steps = routes.reshape(steps_count, step_tokens, TOP)
    return lax.map(jax.checkpoint(one_step), (tokens_steps, routes_steps)).reshape(TOKENS, D)

def reference(hidden_in, norm_attn, w_query, w_key, w_value, w_out, norm_ffn, w_router, w_gate_up, w_down, routes, out_grad):
    floats = jax.tree.map(widen, (hidden_in, norm_attn, w_query, w_key, w_value, w_out, norm_ffn, w_router, w_gate_up, w_down))

    def forward(*weights_in):
        return layer(*weights_in, routes)
    output, pullback = jax.vjp(forward, *floats)
    gradients = pullback(out_grad.astype(jnp.float32))
    return (output.astype(jnp.bfloat16), gradients[0].astype(jnp.bfloat16), gradients[1], gradients[2], gradients[3], gradients[4], gradients[5], gradients[6], gradients[7], gradients[8], gradients[9])
```

```python
from functools import partial

import jax
import jax.numpy as jnp
from jax import lax
from jax.sharding import PartitionSpec as P

HEAD_DIM = 64
EPSILON = 1e-06
RESIDUAL = 0.22
SCORE_SCALE = 0.015625
NEGATIVE = -1e30
F32 = jnp.float32
BF16 = jnp.bfloat16


def rms_scale(values):
    return lax.rsqrt(jnp.mean(values * values, axis=-1, keepdims=True) + EPSILON)


def rotary_tables(length, head_width):
    half_width = head_width // 2
    frequency = 10000.0 ** (-2.0 * jnp.arange(half_width, dtype=F32) / head_width)
    angles = jnp.arange(length, dtype=F32)[:, None] * frequency[None, :]
    return (jnp.cos(angles), jnp.sin(angles))


def rotate(values, cosine, sine_table):
    half_width = values.shape[-1] // 2
    first_half = values[..., :half_width]
    second_half = values[..., half_width:]
    cos_b = cosine[:, None, :]
    sin_b = sine_table[:, None, :]
    return jnp.concatenate(
        [first_half * cos_b - second_half * sin_b, second_half * cos_b + first_half * sin_b],
        axis=-1,
    )


def attention_probs(scores):
    length = scores.shape[-1]
    causal = jnp.arange(length)[:, None] >= jnp.arange(length)[None, :]
    return jax.nn.softmax(jnp.where(causal, scores, NEGATIVE), axis=-1)


def product(left, right):
    return jnp.dot(left, right, preferred_element_type=F32)


def left_product(left_rows, right_rows):
    return lax.dot_general(
        left_rows, right_rows, (((0,), (0,)), ((), ())), preferred_element_type=F32
    )


def right_transposed(left_rows, weight):
    return lax.dot_general(
        left_rows, weight, (((1,), (1,)), ((), ())), preferred_element_type=F32
    )


def shift(values, step):
    n = lax.axis_size("shard")
    return lax.ppermute(values, "shard", [(i, (i + step) % n) for i in range(n)])


def piece(values, index, axis):
    n = lax.axis_size("shard")
    width = values.shape[axis] // n
    return lax.dynamic_slice_in_dim(values, lax.rem(index, n) * width, width, axis)


def rows_of_all(values):
    n = lax.axis_size("shard")
    return jnp.concatenate([values] + [shift(values, d) for d in range(1, n)], axis=0)


def columns_of_all(values):
    n, me = lax.axis_size("shard"), lax.axis_index("shard")
    parts = [piece(values, me, 1)]
    parts += [shift(piece(values, me + d, 1), d) for d in range(1, n)]
    return jnp.concatenate(parts, axis=0)


def sum_home(partial_rows):
    n = lax.axis_size("shard")
    rows = partial_rows.shape[0] // n
    total = partial_rows[:rows]
    for d in range(1, n):
        total = total + shift(partial_rows[d * rows : (d + 1) * rows].astype(BF16), -d).astype(F32)
    return total


def columns_home(values):
    n, me = lax.axis_size("shard"), lax.axis_index("shard")
    rows, width = values.shape[0] // n, values.shape[1]
    parts = [values[:rows]]
    parts += [shift(values[d * rows : (d + 1) * rows], -d) for d in range(1, n)]
    if n == 2:
        return jnp.where(
            me == 0, jnp.concatenate(parts, axis=1), jnp.concatenate(parts[::-1], axis=1)
        )
    return jnp.roll(jnp.concatenate(parts, axis=1), me * width, axis=1)


def sum_pieces(values, axis, sent=BF16):
    n, me = lax.axis_size("shard"), lax.axis_index("shard")
    total = piece(values, me, axis)
    for d in range(1, n):
        total = total + shift(piece(values, me + d, axis).astype(sent), d).astype(F32)
    return total


def shards(
    hidden_in,
    norm_attn,
    w_query,
    w_key,
    w_value,
    w_out,
    norm_ffn,
    w_router,
    w_gate_up,
    w_down,
    routes,
    out_grad,
):
    tokens, model_width = hidden_in.shape
    kv_heads = w_key.shape[1] // HEAD_DIM
    q_heads = w_query.shape[1] // HEAD_DIM
    groups = q_heads // kv_heads
    q_width, kv_width = w_query.shape[1], w_key.shape[1]
    experts = w_router.shape[1]
    w_gu, w_dn = w_gate_up[0], w_down[0]
    ffn = w_dn.shape[0]

    small = lax.all_gather(
        jnp.concatenate([w_router, norm_ffn[:, None]], axis=1), "shard", axis=0, tiled=True
    )
    router_w, gain_two = small[:, :experts], small[:, experts].astype(F32)
    mask = jnp.any(
        routes[:, :, None] == jnp.arange(experts, dtype=jnp.int32)[None, None, :], axis=1
    )
    mask_all = lax.all_gather(mask.astype(BF16), "expert", axis=0, tiled=True)
    og_all = lax.all_gather(out_grad, "expert", axis=0, tiled=True)

    cosine, sine_table = rotary_tables(tokens, HEAD_DIM)
    turning = partial(rotate, cosine=cosine, sine_table=sine_table)
    inputs = hidden_in.astype(F32)
    r1 = rms_scale(inputs)
    gain_one = norm_attn.astype(F32)
    hidden_cols = columns_of_all(hidden_in).astype(F32)
    scaled_cols = hidden_cols * rows_of_all(r1)
    xn_one = (scaled_cols * gain_one).astype(BF16)
    qkv = sum_home(
        jnp.concatenate(
            [product(xn_one, w_query), product(xn_one, w_key), product(xn_one, w_value)], axis=1
        )
    )
    raw_query = qkv[:, :q_width].reshape(tokens, q_heads, HEAD_DIM)
    raw_key = qkv[:, q_width : q_width + kv_width].reshape(tokens, kv_heads, HEAD_DIM)
    value_low = qkv[:, q_width + kv_width :].astype(BF16).reshape(tokens, kv_heads, HEAD_DIM)
    rot_query, query_back = jax.vjp(turning, raw_query)
    rot_key, key_back = jax.vjp(turning, raw_key)
    query_low = rot_query.astype(BF16).reshape(tokens, kv_heads, groups, HEAD_DIM)
    key_low = rot_key.astype(BF16)
    scores = SCORE_SCALE * jnp.einsum(
        "tkgd,skd->kgts", query_low, key_low, preferred_element_type=F32
    )
    probs, probs_back = jax.vjp(attention_probs, scores)
    probs_low = probs.astype(BF16)
    attended = jnp.einsum("kgts,skd->tkgd", probs_low, value_low, preferred_element_type=F32)
    attended = attended.reshape(tokens, q_heads * HEAD_DIM).astype(BF16)
    attended_cols = columns_of_all(attended)
    middle = inputs + RESIDUAL * sum_home(product(attended_cols, w_out))
    r2 = rms_scale(middle)
    xn_two = (middle * r2 * gain_two).astype(BF16)

    x_all = lax.all_gather(xn_two, "expert", axis=0, tiled=True)
    logits_all = jnp.where(mask_all > 0, product(x_all, router_w), NEGATIVE)
    gates_all = jax.nn.softmax(logits_all, axis=-1)
    mine = jnp.arange(experts, dtype=jnp.int32) == lax.axis_index("expert")
    gate = jnp.sum(jnp.where(mine, gates_all, 0.0), axis=-1, keepdims=True)
    gate_up = product(x_all, w_gu)
    g, u = gate_up[:, :ffn], gate_up[:, ffn:]
    sig = jax.nn.sigmoid(g)
    hid = (g * sig * u).astype(BF16)
    y = product(hid, w_dn).astype(BF16).astype(F32)
    mixture = lax.psum_scatter(
        (gate * y).astype(BF16), "expert", scatter_dimension=0, tiled=True
    )
    og_scaled = RESIDUAL * og_all.astype(F32)
    dy = (gate * og_scaled).astype(BF16)
    gate_grad_col = jnp.sum(y * og_scaled, axis=-1).reshape(experts, tokens)
    gate_grad = lax.all_to_all(gate_grad_col, "expert", split_axis=0, concat_axis=0, tiled=True).T
    dhid = right_transposed(dy, w_dn)
    dgu = jnp.concatenate(
        [dhid * u * sig * (1.0 + g * (1.0 - sig)), dhid * g * sig], axis=1
    ).astype(BF16)
    token_grad = lax.psum_scatter(
        right_transposed(dgu, w_gu).astype(BF16), "expert", scatter_dimension=0, tiled=True
    ).astype(F32)
    down_sum = sum_pieces(left_product(hid, dy), 1)
    gate_up_sum = sum_pieces(left_product(x_all, dgu), 1)

    output = (middle + RESIDUAL * mixture.astype(F32)).astype(BF16)
    upstream = out_grad.astype(F32)
    gates = jax.nn.softmax(
        jnp.where(mask, product(xn_two, router_w), NEGATIVE), axis=-1
    )
    gate_grad = jnp.where(mask, gate_grad, 0.0)
    logit_grad = (
        gates * (gate_grad - jnp.sum(gates * gate_grad, axis=-1, keepdims=True))
    ).astype(BF16)
    xn_two_grad = token_grad + right_transposed(logit_grad, router_w)
    scaled_two = middle * r2
    gain_two_grad = jnp.sum(xn_two_grad * scaled_two, axis=0)
    w2 = xn_two_grad * gain_two
    middle_grad = (
        upstream + r2 * (w2 - scaled_two * jnp.mean(w2 * scaled_two, axis=-1, keepdims=True))
    )
    branch_low = (RESIDUAL * middle_grad).astype(BF16)
    router_local = left_product(xn_two, logit_grad)
    branch_all = rows_of_all(branch_low)
    attended_grad = columns_home(right_transposed(branch_all, w_out).astype(BF16))
    output_local = left_product(attended_cols, branch_all).astype(BF16)
    small_local = sum_pieces(
        jnp.concatenate([router_local, gain_two_grad[:, None]], axis=1), 0, F32
    ).astype(BF16)
    small_rows = -(-(experts + 1) // 16) * 16
    small_pad = jnp.pad(
        small_local.T,
        ((0, small_rows - experts - 1), (0, model_width - small_local.shape[0])),
    )
    first_sum = lax.psum(jnp.concatenate([output_local, small_pad], axis=0), "expert").astype(F32)

    attended_grad = attended_grad.reshape(tokens, kv_heads, groups, HEAD_DIM)
    value_grad = jnp.einsum(
        "kgts,tkgd->skd", probs_low, attended_grad, preferred_element_type=F32
    )
    probs_grad = jnp.einsum(
        "tkgd,skd->kgts", attended_grad, value_low, preferred_element_type=F32
    )
    (score_grad,) = probs_back(probs_grad)
    score_low = score_grad.astype(BF16)
    query_grad = SCORE_SCALE * jnp.einsum(
        "kgts,skd->tkgd", score_low, key_low, preferred_element_type=F32
    )
    key_grad = SCORE_SCALE * jnp.einsum(
        "kgts,tkgd->skd", score_low, query_low, preferred_element_type=F32
    )
    (query_raw_grad,) = query_back(query_grad.reshape(tokens, q_heads, HEAD_DIM))
    (key_raw_grad,) = key_back(key_grad)
    qkv_grad = jnp.concatenate(
        [
            query_raw_grad.reshape(tokens, q_width).astype(BF16),
            key_raw_grad.reshape(tokens, kv_width).astype(BF16),
            value_grad.reshape(tokens, kv_width).astype(BF16),
        ],
        axis=1,
    )
    qkv_all = rows_of_all(qkv_grad)
    xn_one_grad = (
        right_transposed(qkv_all[:, :q_width], w_query)
        + right_transposed(qkv_all[:, q_width : q_width + kv_width], w_key)
        + right_transposed(qkv_all[:, q_width + kv_width :], w_value)
    )
    gain_one_grad = jnp.sum(xn_one_grad * scaled_cols, axis=0)
    second = left_product(xn_one, qkv_all).astype(BF16)
    gain_pad = jnp.pad(
        gain_one_grad.astype(BF16)[None, :],
        ((0, 15), (0, second.shape[1] - gain_one_grad.shape[0])),
    )
    second_sum = lax.psum(jnp.concatenate([second, gain_pad], axis=0), "expert").astype(F32)
    w1 = columns_home((xn_one_grad * gain_one).astype(BF16)).astype(F32)
    scaled_one = inputs * r1
    input_grad = (
        middle_grad + r1 * (w1 - scaled_one * jnp.mean(w1 * scaled_one, axis=-1, keepdims=True))
    ).astype(BF16)

    own = norm_attn.shape[0]
    return (
        output,
        input_grad,
        second_sum[own, :own],
        second_sum[:own, :q_width],
        second_sum[:own, q_width : q_width + kv_width],
        second_sum[:own, q_width + kv_width :],
        first_sum[:own],
        first_sum[own + experts, :own],
        first_sum[own : own + experts, :own].T,
        gate_up_sum[None],
        down_sum[None],
    )


def solution(mesh):
    placed = (
        P(("expert", "shard"), None),
        P("shard"),
        P("shard", None),
        P("shard", None),
        P("shard", None),
        P("shard", None),
        P("shard"),
        P("shard", None),
        P("expert", None, None),
        P("expert", None, None),
        P(("expert", "shard"), None),
        P(("expert", "shard"), None),
    )
    return jax.shard_map(
        shards,
        mesh=mesh,
        in_specs=placed,
        out_specs=(
            P(("expert", "shard"), None),
            P(("expert", "shard"), None),
            P("shard"),
            P("shard", None),
            P("shard", None),
            P("shard", None),
            P("shard", None),
            P("shard"),
            P("shard", None),
            P("expert", None, "shard"),
            P("expert", None, "shard"),
        ),
        check_vma=False,
    )
```

```python
from functools import partial

import jax
import jax.numpy as jnp
from jax import lax
from jax.experimental import pallas as pl
from jax.experimental.pallas import tpu as pltpu
from jax.sharding import PartitionSpec as P

HEAD_DIM = 64
EPSILON = 1e-06
RESIDUAL = 0.22
SCORE_SCALE = 0.015625
NEGATIVE = -1e30
F32 = jnp.float32
BF16 = jnp.bfloat16


def rms_scale(values):
    return lax.rsqrt(jnp.mean(values * values, axis=-1, keepdims=True) + EPSILON)


def rotary_tables(length, head_width):
    half_width = head_width // 2
    frequency = 10000.0 ** (-2.0 * jnp.arange(half_width, dtype=F32) / head_width)
    angles = jnp.arange(length, dtype=F32)[:, None] * frequency[None, :]
    return (jnp.cos(angles), jnp.sin(angles))


def rotate(values, cosine, sine_table):
    half_width = values.shape[-1] // 2
    first_half = values[..., :half_width]
    second_half = values[..., half_width:]
    cos_b = cosine[:, None, :]
    sin_b = sine_table[:, None, :]
    return jnp.concatenate(
        [first_half * cos_b - second_half * sin_b, second_half * cos_b + first_half * sin_b],
        axis=-1,
    )


def attention_probs(scores):
    length = scores.shape[-1]
    causal = jnp.arange(length)[:, None] >= jnp.arange(length)[None, :]
    return jax.nn.softmax(jnp.where(causal, scores, NEGATIVE), axis=-1)


def product(left, right):
    return jnp.dot(left, right, preferred_element_type=F32)


def left_product(left_rows, right_rows):
    return lax.dot_general(
        left_rows, right_rows, (((0,), (0,)), ((), ())), preferred_element_type=F32
    )


def right_transposed(left_rows, weight):
    return lax.dot_general(
        left_rows, weight, (((1,), (1,)), ((), ())), preferred_element_type=F32
    )


def shift(values, step):
    n = lax.axis_size("shard")
    return lax.ppermute(values, "shard", [(i, (i + step) % n) for i in range(n)])


def piece(values, index, axis):
    n = lax.axis_size("shard")
    width = values.shape[axis] // n
    return lax.dynamic_slice_in_dim(values, lax.rem(index, n) * width, width, axis)


def rows_of_all(values):
    n = lax.axis_size("shard")
    return jnp.concatenate([values] + [shift(values, d) for d in range(1, n)], axis=0)


def rows_in_order(values):
    n, me = lax.axis_size("shard"), lax.axis_index("shard")
    parts = [values] + [shift(values, -d) for d in range(1, n)]
    if n == 2:
        return jnp.where(me == 0, jnp.concatenate(parts), jnp.concatenate(parts[::-1]))
    return jnp.roll(jnp.concatenate(parts), me * values.shape[0], axis=0)


def columns_of_all(values):
    n, me = lax.axis_size("shard"), lax.axis_index("shard")
    parts = [piece(values, me, 1)]
    parts += [shift(piece(values, me + d, 1), d) for d in range(1, n)]
    return jnp.concatenate(parts, axis=0)


def sum_home(partial_rows):
    n = lax.axis_size("shard")
    rows = partial_rows.shape[0] // n
    total = partial_rows[:rows]
    for d in range(1, n):
        total = total + shift(partial_rows[d * rows : (d + 1) * rows].astype(BF16), -d).astype(F32)
    return total


def columns_home(values):
    n, me = lax.axis_size("shard"), lax.axis_index("shard")
    rows, width = values.shape[0] // n, values.shape[1]
    parts = [values[:rows]]
    parts += [shift(values[d * rows : (d + 1) * rows], -d) for d in range(1, n)]
    if n == 2:
        return jnp.where(
            me == 0, jnp.concatenate(parts, axis=1), jnp.concatenate(parts[::-1], axis=1)
        )
    return jnp.roll(jnp.concatenate(parts, axis=1), me * width, axis=1)


def sum_pieces(values, axis, sent=BF16):
    n, me = lax.axis_size("shard"), lax.axis_index("shard")
    total = piece(values, me, axis)
    for d in range(1, n):
        total = total + shift(piece(values, me + d, axis).astype(sent), d).astype(F32)
    return total


MESH = pl.DeviceIdType.MESH


def grid_of(n):
    return (4, n // 8) if n % 8 == 0 else (n // 2, 1)


class Place:
    def __init__(self, n):
        self.outer, self.inner = grid_of(n)
        me = lax.axis_index("expert")
        self.me = me
        self.core = lax.rem(me, 2)
        self.b = lax.rem(me // 2, self.inner)
        self.a = me // (2 * self.inner)

    def index(self, da=0, db=0, dc=0):
        a = lax.rem(self.a + da, self.outer)
        b = lax.rem(self.b + db, self.inner)
        return (a * self.inner + b) * 2 + lax.rem(self.core + dc, 2)

    def barrier(self):
        sem = pltpu.get_barrier_semaphore()
        mates = [self.index(da=d) for d in range(1, self.outer)]
        mates += [self.index(db=d) for d in range(1, self.inner)]
        mates += [self.index(dc=1)]
        for mate in mates:
            pl.semaphore_signal(sem, inc=1, device_id={"expert": mate}, device_id_type=MESH)
        pl.semaphore_wait(sem, len(mates))


def remote(src, dst, send_sem, recv_sem, target):
    return pltpu.make_async_remote_copy(
        src_ref=src,
        dst_ref=dst,
        send_sem=send_sem,
        recv_sem=recv_sem,
        device_id={"expert": target},
        device_id_type=MESH,
    )


def gather_steps(place, sources, outs, local_sem, send_sem, recv_sem):
    outer, inner = place.outer, place.inner
    items = range(len(sources))
    started = []

    def send(block, target, number, own=False):
        for i in items:
            src = sources[i] if own else outs[i].at[block]
            copy = remote(
                src, outs[i].at[block], send_sem.at[i, number], recv_sem.at[i, block], target
            )
            copy.start()
            started.append(copy)

    def arrived(block):
        for i in items:
            remote(
                outs[i].at[block], outs[i].at[block], send_sem.at[i, 0], recv_sem.at[i, block], place.index(dc=1)
            ).wait_recv()

    number = 0
    for d in range(1, outer):
        send(place.me, place.index(da=d), number, True)
        number += 1
    for d in range(1, inner):
        send(place.me, place.index(db=d), number, True)
        number += 1
    send(place.me, place.index(dc=1), number, True)
    number += 1
    local = [
        pltpu.make_async_copy(sources[i], outs[i].at[place.me], local_sem.at[i]) for i in items
    ]
    for copy in local:
        copy.start()
    for da in range(1, outer):
        block = place.index(da=da)
        arrived(block)
        for d in range(1, inner):
            send(block, place.index(db=d), number)
            number += 1
        send(block, place.index(dc=1), number)
        number += 1
    for db in range(1, inner):
        for da in range(outer):
            block = place.index(da=da, db=db)
            arrived(block)
            send(block, place.index(dc=1), number)
            number += 1
    for da in range(outer):
        for db in range(inner):
            arrived(place.index(da=da, db=db, dc=1))
    for copy in started:
        copy.wait_send()
    for copy in local:
        copy.wait()


def gather_sends(n):
    outer, inner = grid_of(n)
    return (outer - 1) + outer * (inner - 1) + outer * inner


def scatter_steps(place, src, buf_c, buf_b, buf_a, sems):
    outer, inner = place.outer, place.inner
    send_c, recv_c, send_b, recv_b, send_a, recv_a = sems
    far_first = list(range(1, outer)) + [0]
    inner_order = list(range(1, inner)) + [0]
    started = []

    def across(da, db):
        slot = place.index(da=da, db=db) // 2
        return remote(
            src.at[place.index(da=da, db=db, dc=1)],
            buf_c.at[slot],
            send_c.at[slot],
            recv_c.at[slot],
            place.index(dc=1),
        )

    def along_inner(da, db):
        slot = place.index(da=da, db=db) // 2
        a = lax.rem(place.a + da, outer)
        return remote(
            buf_c.at[slot],
            buf_b.at[db - 1, a],
            send_b.at[db - 1, a],
            recv_b.at[db - 1, a],
            place.index(db=db),
        )

    def along_outer(da):
        slot = place.index(da=da) // 2
        return remote(
            buf_c.at[slot], buf_a.at[da - 1], send_a.at[da - 1], recv_a.at[da - 1], place.index(da=da)
        )

    def start(copy):
        copy.start()
        started.append(copy)

    for db in inner_order:
        for da in far_first:
            start(across(da, db))
    for db in inner_order:
        for da in far_first:
            slot = place.index(da=da, db=db) // 2
            across(da, db).wait_recv()
            block = place.index(da=da, db=db)
            buf_c[slot] = (buf_c[slot].astype(F32) + src[block].astype(F32)).astype(BF16)
            if db:
                start(along_inner(da, db))
    total = None
    for da in far_first:
        slot = place.index(da=da) // 2
        a = lax.rem(place.a + da, outer)
        total = buf_c[slot].astype(F32)
        for db in range(1, inner):
            along_inner(da, db).wait_recv()
            total = total + buf_b[db - 1, a].astype(F32)
        if da:
            buf_c[slot] = total.astype(BF16)
            start(along_outer(da))
    for da in range(1, outer):
        along_outer(da).wait_recv()
        total = total + buf_a[da - 1].astype(F32)
    for copy in started:
        copy.wait_send()
    return total


def scatter_scratch(n, rows, width):
    outer, inner = grid_of(n)
    dma = pltpu.SemaphoreType.DMA
    inner_slots = max(1, inner - 1)
    return [
        pltpu.VMEM((outer * inner, rows, width), BF16),
        pltpu.VMEM((inner_slots, outer, rows, width), BF16),
        pltpu.VMEM((outer - 1, rows, width), BF16),
        dma((outer * inner,)),
        dma((outer * inner,)),
        dma((inner_slots, outer)),
        dma((inner_slots, outer)),
        dma((outer - 1,)),
        dma((outer - 1,)),
    ]


def kernel_params(number):
    return pltpu.CompilerParams(
        collective_id=number, has_side_effects=True, vmem_limit_bytes=48 * 1024 * 1024
    )


def gather_kernel(n, count, *refs):
    place = Place(n)
    place.barrier()
    gather_steps(place, refs[:count], refs[count : 2 * count], *refs[2 * count :])


def gather_expert(arrays, number):
    n, count = lax.axis_size("expert"), len(arrays)
    dma = pltpu.SemaphoreType.DMA
    outs = pl.pallas_call(
        partial(gather_kernel, n, count),
        out_shape=[jax.ShapeDtypeStruct((n,) + v.shape, v.dtype) for v in arrays],
        in_specs=[pl.BlockSpec(memory_space=pl.ANY)] * count,
        out_specs=[pl.BlockSpec(memory_space=pl.ANY)] * count,
        scratch_shapes=[dma((count,)), dma((count, gather_sends(n))), dma((count, n))],
        compiler_params=kernel_params(number),
    )(*arrays)
    return [out.reshape((-1,) + v.shape[1:]) for out, v in zip(outs, arrays)]


def scatter_kernel(n, src, out, buf_c, buf_b, buf_a, *sems):
    place = Place(n)
    place.barrier()
    out[...] = scatter_steps(place, src, buf_c, buf_b, buf_a, sems)


def scatter_expert(values, number):
    n = lax.axis_size("expert")
    rows, width = values.shape[0] // n, values.shape[1]
    return pl.pallas_call(
        partial(scatter_kernel, n),
        out_shape=jax.ShapeDtypeStruct((rows, width), F32),
        in_specs=[pl.BlockSpec(memory_space=pltpu.VMEM)],
        out_specs=pl.BlockSpec(memory_space=pltpu.VMEM),
        scratch_shapes=scatter_scratch(n, rows, width),
        compiler_params=kernel_params(number),
    )(values.reshape(n, rows, width))


def sum_kernel(n, src, out, own, buf_c, buf_b, buf_a, *sems):
    place = Place(n)
    place.barrier()
    own[...] = scatter_steps(place, src, buf_c, buf_b, buf_a, sems[:6]).astype(BF16)
    gather_steps(place, [own], [out], *sems[6:])


def sum_expert(values, number):
    n = lax.axis_size("expert")
    dma = pltpu.SemaphoreType.DMA
    whole_rows, width = values.shape
    rows = -(-whole_rows // (16 * n)) * 16
    values = jnp.pad(values, ((0, rows * n - whole_rows), (0, 0)))
    out = pl.pallas_call(
        partial(sum_kernel, n),
        out_shape=jax.ShapeDtypeStruct((n, rows, width), BF16),
        in_specs=[pl.BlockSpec(memory_space=pltpu.VMEM)],
        out_specs=pl.BlockSpec(memory_space=pl.ANY),
        scratch_shapes=[pltpu.VMEM((rows, width), BF16)]
        + scatter_scratch(n, rows, width)
        + [dma((1,)), dma((1, gather_sends(n))), dma((1, n))],
        compiler_params=kernel_params(number),
    )(values.reshape(n, rows, width))
    return out.reshape(n * rows, width)[:whole_rows]


def shards(
    hidden_in,
    norm_attn,
    w_query,
    w_key,
    w_value,
    w_out,
    norm_ffn,
    w_router,
    w_gate_up,
    w_down,
    routes,
    out_grad,
):
    tokens, model_width = hidden_in.shape
    kv_heads = w_key.shape[1] // HEAD_DIM
    q_heads = w_query.shape[1] // HEAD_DIM
    groups = q_heads // kv_heads
    q_width, kv_width = w_query.shape[1], w_key.shape[1]
    experts = w_router.shape[1]
    w_gu, w_dn = w_gate_up[0], w_down[0]
    ffn = w_dn.shape[0]

    small = rows_in_order(jnp.concatenate([w_router, norm_ffn[:, None]], axis=1))
    router_w, gain_two = small[:, :experts], small[:, experts].astype(F32)
    mask = jnp.any(
        routes[:, :, None] == jnp.arange(experts, dtype=jnp.int32)[None, None, :], axis=1
    )
    og_all = lax.all_gather(out_grad, "expert", axis=0, tiled=True)

    cosine, sine_table = rotary_tables(tokens, HEAD_DIM)
    turning = partial(rotate, cosine=cosine, sine_table=sine_table)
    inputs = hidden_in.astype(F32)
    r1 = rms_scale(inputs)
    gain_one = norm_attn.astype(F32)
    hidden_cols = columns_of_all(hidden_in).astype(F32)
    scaled_cols = hidden_cols * rows_of_all(r1)
    xn_one = (scaled_cols * gain_one).astype(BF16)
    qkv = sum_home(
        jnp.concatenate(
            [product(xn_one, w_query), product(xn_one, w_key), product(xn_one, w_value)], axis=1
        )
    )
    raw_query = qkv[:, :q_width].reshape(tokens, q_heads, HEAD_DIM)
    raw_key = qkv[:, q_width : q_width + kv_width].reshape(tokens, kv_heads, HEAD_DIM)
    value_low = qkv[:, q_width + kv_width :].astype(BF16).reshape(tokens, kv_heads, HEAD_DIM)
    rot_query, query_back = jax.vjp(turning, raw_query)
    rot_key, key_back = jax.vjp(turning, raw_key)
    query_low = rot_query.astype(BF16).reshape(tokens, kv_heads, groups, HEAD_DIM)
    key_low = rot_key.astype(BF16)
    scores = SCORE_SCALE * jnp.einsum(
        "tkgd,skd->kgts", query_low, key_low, preferred_element_type=F32
    )
    probs, probs_back = jax.vjp(attention_probs, scores)
    probs_low = probs.astype(BF16)
    attended = jnp.einsum("kgts,skd->tkgd", probs_low, value_low, preferred_element_type=F32)
    attended = attended.reshape(tokens, q_heads * HEAD_DIM).astype(BF16)
    attended_cols = columns_of_all(attended)
    middle = inputs + RESIDUAL * sum_home(product(attended_cols, w_out))
    r2 = rms_scale(middle)
    xn_two = (middle * r2 * gain_two).astype(BF16)

    mask_pad = jnp.pad(mask.astype(BF16), ((0, 0), (0, -experts % 128)))
    x_all, mask_all = gather_expert([xn_two, mask_pad], 1)
    mask_all = mask_all[:, :experts]
    logits_all = jnp.where(mask_all > 0, product(x_all, router_w), NEGATIVE)
    gates_all = jax.nn.softmax(logits_all, axis=-1)
    mine = jnp.arange(experts, dtype=jnp.int32) == lax.axis_index("expert")
    gate = jnp.sum(jnp.where(mine, gates_all, 0.0), axis=-1, keepdims=True)
    gate_up = product(x_all, w_gu)
    g, u = gate_up[:, :ffn], gate_up[:, ffn:]
    sig = jax.nn.sigmoid(g)
    hid = (g * sig * u).astype(BF16)
    y = product(hid, w_dn).astype(BF16).astype(F32)
    mixture = lax.psum_scatter(
        (gate * y).astype(BF16), "expert", scatter_dimension=0, tiled=True
    )
    og_scaled = RESIDUAL * og_all.astype(F32)
    dy = (gate * og_scaled).astype(BF16)
    gate_grad_col = jnp.sum(y * og_scaled, axis=-1).reshape(experts, tokens)
    gate_grad = lax.all_to_all(gate_grad_col, "expert", split_axis=0, concat_axis=0, tiled=True).T
    dhid = right_transposed(dy, w_dn)
    dgu = jnp.concatenate(
        [dhid * u * sig * (1.0 + g * (1.0 - sig)), dhid * g * sig], axis=1
    ).astype(BF16)
    token_grad = scatter_expert(right_transposed(dgu, w_gu).astype(BF16), 2)
    down_sum = sum_pieces(left_product(hid, dy), 1)
    gate_up_sum = sum_pieces(left_product(x_all, dgu), 1)

    output = (middle + RESIDUAL * mixture.astype(F32)).astype(BF16)
    upstream = out_grad.astype(F32)
    gates = jax.nn.softmax(
        jnp.where(mask, product(xn_two, router_w), NEGATIVE), axis=-1
    )
    gate_grad = jnp.where(mask, gate_grad, 0.0)
    logit_grad = (
        gates * (gate_grad - jnp.sum(gates * gate_grad, axis=-1, keepdims=True))
    ).astype(BF16)
    xn_two_grad = token_grad + right_transposed(logit_grad, router_w)
    scaled_two = middle * r2
    gain_two_grad = jnp.sum(xn_two_grad * scaled_two, axis=0)
    w2 = xn_two_grad * gain_two
    middle_grad = (
        upstream + r2 * (w2 - scaled_two * jnp.mean(w2 * scaled_two, axis=-1, keepdims=True))
    )
    branch_low = (RESIDUAL * middle_grad).astype(BF16)
    router_local = left_product(xn_two, logit_grad)
    branch_all = rows_of_all(branch_low)
    attended_grad = columns_home(right_transposed(branch_all, w_out).astype(BF16))
    output_local = left_product(attended_cols, branch_all).astype(BF16)
    small_local = sum_pieces(
        jnp.concatenate([router_local, gain_two_grad[:, None]], axis=1), 0, F32
    )

    attended_grad = attended_grad.reshape(tokens, kv_heads, groups, HEAD_DIM)
    value_grad = jnp.einsum(
        "kgts,tkgd->skd", probs_low, attended_grad, preferred_element_type=F32
    )
    probs_grad = jnp.einsum(
        "tkgd,skd->kgts", attended_grad, value_low, preferred_element_type=F32
    )
    (score_grad,) = probs_back(probs_grad)
    score_low = score_grad.astype(BF16)
    query_grad = SCORE_SCALE * jnp.einsum(
        "kgts,skd->tkgd", score_low, key_low, preferred_element_type=F32
    )
    key_grad = SCORE_SCALE * jnp.einsum(
        "kgts,tkgd->skd", score_low, query_low, preferred_element_type=F32
    )
    (query_raw_grad,) = query_back(query_grad.reshape(tokens, q_heads, HEAD_DIM))
    (key_raw_grad,) = key_back(key_grad)
    qkv_grad = jnp.concatenate(
        [
            query_raw_grad.reshape(tokens, q_width).astype(BF16),
            key_raw_grad.reshape(tokens, kv_width).astype(BF16),
            value_grad.reshape(tokens, kv_width).astype(BF16),
        ],
        axis=1,
    )
    qkv_all = rows_of_all(qkv_grad)
    xn_one_grad = (
        right_transposed(qkv_all[:, :q_width], w_query)
        + right_transposed(qkv_all[:, q_width : q_width + kv_width], w_key)
        + right_transposed(qkv_all[:, q_width + kv_width :], w_value)
    )
    gain_one_grad = jnp.sum(xn_one_grad * scaled_cols, axis=0)
    small_local = jnp.concatenate([small_local, gain_one_grad[:, None]], axis=1)
    small_pad = jnp.pad(small_local, ((0, 0), (0, -small_local.shape[1] % 128)))
    sums = sum_expert(
        jnp.concatenate(
            [left_product(xn_one, qkv_all).astype(BF16), output_local, small_pad.astype(BF16)],
            axis=1,
        ),
        3,
    ).astype(F32)
    w1 = columns_home((xn_one_grad * gain_one).astype(BF16)).astype(F32)
    scaled_one = inputs * r1
    input_grad = (
        middle_grad + r1 * (w1 - scaled_one * jnp.mean(w1 * scaled_one, axis=-1, keepdims=True))
    ).astype(BF16)

    out_at = q_width + 2 * kv_width
    small_at = out_at + model_width
    return (
        output,
        input_grad,
        sums[:, small_at + experts + 1],
        sums[:, :q_width],
        sums[:, q_width : q_width + kv_width],
        sums[:, q_width + kv_width : out_at],
        sums[:, out_at:small_at],
        sums[:, small_at + experts],
        sums[:, small_at : small_at + experts],
        gate_up_sum[None],
        down_sum[None],
    )


def solution(mesh):
    placed = (
        P(("expert", "shard"), None),
        P("shard"),
        P("shard", None),
        P("shard", None),
        P("shard", None),
        P("shard", None),
        P("shard"),
        P("shard", None),
        P("expert", None, None),
        P("expert", None, None),
        P(("expert", "shard"), None),
        P(("expert", "shard"), None),
    )
    return jax.shard_map(
        shards,
        mesh=mesh,
        in_specs=placed,
        out_specs=(
            P(("expert", "shard"), None),
            P(("expert", "shard"), None),
            P("shard"),
            P("shard", None),
            P("shard", None),
            P("shard", None),
            P("shard", None),
            P("shard"),
            P("shard", None),
            P("expert", None, "shard"),
            P("expert", None, "shard"),
        ),
        check_vma=False,
    )
```

```python
from functools import partial

import jax
import jax.numpy as jnp
from jax import lax
from jax.experimental import pallas as pl
from jax.experimental.pallas import tpu as pltpu
from jax.sharding import PartitionSpec as P

HEAD_DIM = 64
EPSILON = 1e-06
RESIDUAL = 0.22
SCORE_SCALE = 0.015625
NEGATIVE = -1e30
F32 = jnp.float32
BF16 = jnp.bfloat16


def rms_scale(values):
    return lax.rsqrt(jnp.mean(values * values, axis=-1, keepdims=True) + EPSILON)


def rotary_tables(length, head_width):
    half_width = head_width // 2
    frequency = 10000.0 ** (-2.0 * jnp.arange(half_width, dtype=F32) / head_width)
    angles = jnp.arange(length, dtype=F32)[:, None] * frequency[None, :]
    return (jnp.cos(angles), jnp.sin(angles))


def rotate(values, cosine, sine_table):
    half_width = values.shape[-1] // 2
    first_half = values[..., :half_width]
    second_half = values[..., half_width:]
    cos_b = cosine[:, None, :]
    sin_b = sine_table[:, None, :]
    return jnp.concatenate(
        [first_half * cos_b - second_half * sin_b, second_half * cos_b + first_half * sin_b],
        axis=-1,
    )


def attention_probs(scores):
    length = scores.shape[-1]
    causal = jnp.arange(length)[:, None] >= jnp.arange(length)[None, :]
    return jax.nn.softmax(jnp.where(causal, scores, NEGATIVE), axis=-1)


def product(left, right):
    return jnp.dot(left, right, preferred_element_type=F32)


def left_product(left_rows, right_rows):
    return lax.dot_general(
        left_rows, right_rows, (((0,), (0,)), ((), ())), preferred_element_type=F32
    )


def right_transposed(left_rows, weight):
    return lax.dot_general(
        left_rows, weight, (((1,), (1,)), ((), ())), preferred_element_type=F32
    )


def shift(values, step):
    n = lax.axis_size("shard")
    return lax.ppermute(values, "shard", [(i, (i + step) % n) for i in range(n)])


def piece(values, index, axis):
    n = lax.axis_size("shard")
    width = values.shape[axis] // n
    return lax.dynamic_slice_in_dim(values, lax.rem(index, n) * width, width, axis)


def rows_of_all(values):
    n = lax.axis_size("shard")
    return jnp.concatenate([values] + [shift(values, d) for d in range(1, n)], axis=0)


def rows_in_order(values):
    n, me = lax.axis_size("shard"), lax.axis_index("shard")
    parts = [values] + [shift(values, -d) for d in range(1, n)]
    if n == 2:
        return jnp.where(me == 0, jnp.concatenate(parts), jnp.concatenate(parts[::-1]))
    return jnp.roll(jnp.concatenate(parts), me * values.shape[0], axis=0)


def columns_of_all(values):
    n, me = lax.axis_size("shard"), lax.axis_index("shard")
    parts = [piece(values, me, 1)]
    parts += [shift(piece(values, me + d, 1), d) for d in range(1, n)]
    return jnp.concatenate(parts, axis=0)


def sum_home(partial_rows):
    n = lax.axis_size("shard")
    rows = partial_rows.shape[0] // n
    total = partial_rows[:rows]
    for d in range(1, n):
        total = total + shift(partial_rows[d * rows : (d + 1) * rows].astype(BF16), -d).astype(F32)
    return total


def columns_home(values):
    n, me = lax.axis_size("shard"), lax.axis_index("shard")
    rows, width = values.shape[0] // n, values.shape[1]
    parts = [values[:rows]]
    parts += [shift(values[d * rows : (d + 1) * rows], -d) for d in range(1, n)]
    if n == 2:
        return jnp.where(
            me == 0, jnp.concatenate(parts, axis=1), jnp.concatenate(parts[::-1], axis=1)
        )
    return jnp.roll(jnp.concatenate(parts, axis=1), me * width, axis=1)


def sum_pieces(values, axis, sent=BF16):
    n, me = lax.axis_size("shard"), lax.axis_index("shard")
    total = piece(values, me, axis)
    for d in range(1, n):
        total = total + shift(piece(values, me + d, axis).astype(sent), d).astype(F32)
    return total


MESH = pl.DeviceIdType.MESH


def grid_of(n):
    return (4, n // 8) if n % 8 == 0 else (n // 2, 1)


class Place:
    def __init__(self, n):
        self.outer, self.inner = grid_of(n)
        me = lax.axis_index("expert")
        self.me = me
        self.core = lax.rem(me, 2)
        self.b = lax.rem(me // 2, self.inner)
        self.a = me // (2 * self.inner)

    def index(self, da=0, db=0, dc=0):
        a = lax.rem(self.a + da, self.outer)
        b = lax.rem(self.b + db, self.inner)
        return (a * self.inner + b) * 2 + lax.rem(self.core + dc, 2)

    def barrier(self):
        sem = pltpu.get_barrier_semaphore()
        mates = [self.index(da=d) for d in range(1, self.outer)]
        mates += [self.index(db=d) for d in range(1, self.inner)]
        mates += [self.index(dc=1)]
        for mate in mates:
            pl.semaphore_signal(sem, inc=1, device_id={"expert": mate}, device_id_type=MESH)
        pl.semaphore_wait(sem, len(mates))


def remote(src, dst, send_sem, recv_sem, target):
    return pltpu.make_async_remote_copy(
        src_ref=src,
        dst_ref=dst,
        send_sem=send_sem,
        recv_sem=recv_sem,
        device_id={"expert": target},
        device_id_type=MESH,
    )


def gather_steps(place, sources, outs, local_sem, send_sem, recv_sem):
    outer, inner = place.outer, place.inner
    items = range(len(sources))
    started = []

    def send(block, target, number, own=False):
        for i in items:
            src = sources[i] if own else outs[i].at[block]
            copy = remote(
                src, outs[i].at[block], send_sem.at[i, number], recv_sem.at[i, block], target
            )
            copy.start()
            started.append(copy)

    def arrived(block):
        for i in items:
            remote(
                outs[i].at[block], outs[i].at[block], send_sem.at[i, 0], recv_sem.at[i, block], place.index(dc=1)
            ).wait_recv()

    number = 0
    for d in range(1, outer):
        send(place.me, place.index(da=d), number, True)
        number += 1
    for d in range(1, inner):
        send(place.me, place.index(db=d), number, True)
        number += 1
    send(place.me, place.index(dc=1), number, True)
    number += 1
    local = [
        pltpu.make_async_copy(sources[i], outs[i].at[place.me], local_sem.at[i]) for i in items
    ]
    for copy in local:
        copy.start()
    for da in range(1, outer):
        block = place.index(da=da)
        arrived(block)
        for d in range(1, inner):
            send(block, place.index(db=d), number)
            number += 1
        send(block, place.index(dc=1), number)
        number += 1
    for db in range(1, inner):
        for da in range(outer):
            block = place.index(da=da, db=db)
            arrived(block)
            send(block, place.index(dc=1), number)
            number += 1
    for da in range(outer):
        for db in range(inner):
            arrived(place.index(da=da, db=db, dc=1))
    for copy in started:
        copy.wait_send()
    for copy in local:
        copy.wait()


def gather_sends(n):
    outer, inner = grid_of(n)
    return (outer - 1) + outer * (inner - 1) + outer * inner


def scatter_steps(place, src, buf_c, buf_b, buf_a, sems):
    outer, inner = place.outer, place.inner
    send_c, recv_c, send_b, recv_b, send_a, recv_a = sems
    far_first = list(range(1, outer)) + [0]
    inner_order = list(range(1, inner)) + [0]
    started = []

    def across(da, db):
        slot = place.index(da=da, db=db) // 2
        return remote(
            src.at[place.index(da=da, db=db, dc=1)],
            buf_c.at[slot],
            send_c.at[slot],
            recv_c.at[slot],
            place.index(dc=1),
        )

    def along_inner(da, db):
        slot = place.index(da=da, db=db) // 2
        a = lax.rem(place.a + da, outer)
        return remote(
            buf_c.at[slot],
            buf_b.at[db - 1, a],
            send_b.at[db - 1, a],
            recv_b.at[db - 1, a],
            place.index(db=db),
        )

    def along_outer(da):
        slot = place.index(da=da) // 2
        return remote(
            buf_c.at[slot], buf_a.at[da - 1], send_a.at[da - 1], recv_a.at[da - 1], place.index(da=da)
        )

    def start(copy):
        copy.start()
        started.append(copy)

    for db in inner_order:
        for da in far_first:
            start(across(da, db))
    for db in inner_order:
        for da in far_first:
            slot = place.index(da=da, db=db) // 2
            across(da, db).wait_recv()
            block = place.index(da=da, db=db)
            buf_c[slot] = (buf_c[slot].astype(F32) + src[block].astype(F32)).astype(BF16)
            if db:
                start(along_inner(da, db))
    total = None
    for da in far_first:
        slot = place.index(da=da) // 2
        a = lax.rem(place.a + da, outer)
        total = buf_c[slot].astype(F32)
        for db in range(1, inner):
            along_inner(da, db).wait_recv()
            total = total + buf_b[db - 1, a].astype(F32)
        if da:
            buf_c[slot] = total.astype(BF16)
            start(along_outer(da))
    for da in range(1, outer):
        along_outer(da).wait_recv()
        total = total + buf_a[da - 1].astype(F32)
    for copy in started:
        copy.wait_send()
    return total


def scatter_scratch(n, rows, width):
    outer, inner = grid_of(n)
    dma = pltpu.SemaphoreType.DMA
    inner_slots = max(1, inner - 1)
    return [
        pltpu.VMEM((outer * inner, rows, width), BF16),
        pltpu.VMEM((inner_slots, outer, rows, width), BF16),
        pltpu.VMEM((outer - 1, rows, width), BF16),
        dma((outer * inner,)),
        dma((outer * inner,)),
        dma((inner_slots, outer)),
        dma((inner_slots, outer)),
        dma((outer - 1,)),
        dma((outer - 1,)),
    ]


def kernel_params(number):
    return pltpu.CompilerParams(
        collective_id=number, has_side_effects=True, vmem_limit_bytes=48 * 1024 * 1024
    )


def gather_kernel(n, count, *refs):
    place = Place(n)
    place.barrier()
    gather_steps(place, refs[:count], refs[count : 2 * count], *refs[2 * count :])


def gather_expert(arrays, number):
    n, count = lax.axis_size("expert"), len(arrays)
    dma = pltpu.SemaphoreType.DMA
    outs = pl.pallas_call(
        partial(gather_kernel, n, count),
        out_shape=[jax.ShapeDtypeStruct((n,) + v.shape, v.dtype) for v in arrays],
        in_specs=[pl.BlockSpec(memory_space=pl.ANY)] * count,
        out_specs=[pl.BlockSpec(memory_space=pl.ANY)] * count,
        scratch_shapes=[dma((count,)), dma((count, gather_sends(n))), dma((count, n))],
        compiler_params=kernel_params(number),
    )(*arrays)
    return [out.reshape((-1,) + v.shape[1:]) for out, v in zip(outs, arrays)]


def scatter_kernel(n, src, out, buf_c, buf_b, buf_a, *sems):
    place = Place(n)
    place.barrier()
    out[...] = scatter_steps(place, src, buf_c, buf_b, buf_a, sems)


def scatter_expert(values, number):
    n = lax.axis_size("expert")
    rows, width = values.shape[0] // n, values.shape[1]
    return pl.pallas_call(
        partial(scatter_kernel, n),
        out_shape=jax.ShapeDtypeStruct((rows, width), F32),
        in_specs=[pl.BlockSpec(memory_space=pltpu.VMEM)],
        out_specs=pl.BlockSpec(memory_space=pltpu.VMEM),
        scratch_shapes=scatter_scratch(n, rows, width),
        compiler_params=kernel_params(number),
    )(values.reshape(n, rows, width))


def sum_kernel(n, src, out, own, buf_c, buf_b, buf_a, *sems):
    place = Place(n)
    place.barrier()
    own[...] = scatter_steps(place, src, buf_c, buf_b, buf_a, sems[:6]).astype(BF16)
    gather_steps(place, [own], [out], *sems[6:])


def sum_expert(values, number):
    n = lax.axis_size("expert")
    dma = pltpu.SemaphoreType.DMA
    whole_rows, width = values.shape
    rows = -(-whole_rows // (16 * n)) * 16
    values = jnp.pad(values, ((0, rows * n - whole_rows), (0, 0)))
    out = pl.pallas_call(
        partial(sum_kernel, n),
        out_shape=jax.ShapeDtypeStruct((n, rows, width), BF16),
        in_specs=[pl.BlockSpec(memory_space=pltpu.VMEM)],
        out_specs=pl.BlockSpec(memory_space=pl.ANY),
        scratch_shapes=[pltpu.VMEM((rows, width), BF16)]
        + scatter_scratch(n, rows, width)
        + [dma((1,)), dma((1, gather_sends(n))), dma((1, n))],
        compiler_params=kernel_params(number),
    )(values.reshape(n, rows, width))
    return out.reshape(n * rows, width)[:whole_rows]


def shards(
    hidden_in,
    norm_attn,
    w_query,
    w_key,
    w_value,
    w_out,
    norm_ffn,
    w_router,
    w_gate_up,
    w_down,
    routes,
    out_grad,
):
    tokens, model_width = hidden_in.shape
    kv_heads = w_key.shape[1] // HEAD_DIM
    q_heads = w_query.shape[1] // HEAD_DIM
    groups = q_heads // kv_heads
    q_width, kv_width = w_query.shape[1], w_key.shape[1]
    experts = w_router.shape[1]
    w_gu, w_dn = w_gate_up[0], w_down[0]
    ffn = w_dn.shape[0]

    small = rows_in_order(jnp.concatenate([w_router, norm_ffn[:, None]], axis=1))
    router_w, gain_two = small[:, :experts], small[:, experts].astype(F32)
    mask = jnp.any(
        routes[:, :, None] == jnp.arange(experts, dtype=jnp.int32)[None, None, :], axis=1
    )
    og_all = lax.all_gather(out_grad, "expert", axis=0, tiled=True)

    cosine, sine_table = rotary_tables(tokens, HEAD_DIM)
    turning = partial(rotate, cosine=cosine, sine_table=sine_table)
    inputs = hidden_in.astype(F32)
    r1 = rms_scale(inputs)
    gain_one = norm_attn.astype(F32)
    hidden_cols = columns_of_all(hidden_in).astype(F32)
    scaled_cols = hidden_cols * rows_of_all(r1)
    xn_one = (scaled_cols * gain_one).astype(BF16)
    qkv = sum_home(
        jnp.concatenate(
            [product(xn_one, w_query), product(xn_one, w_key), product(xn_one, w_value)], axis=1
        )
    )
    raw_query = qkv[:, :q_width].reshape(tokens, q_heads, HEAD_DIM)
    raw_key = qkv[:, q_width : q_width + kv_width].reshape(tokens, kv_heads, HEAD_DIM)
    value_low = qkv[:, q_width + kv_width :].astype(BF16).reshape(tokens, kv_heads, HEAD_DIM)
    rot_query, query_back = jax.vjp(turning, raw_query)
    rot_key, key_back = jax.vjp(turning, raw_key)
    query_low = rot_query.astype(BF16).reshape(tokens, kv_heads, groups, HEAD_DIM)
    key_low = rot_key.astype(BF16)
    scores = SCORE_SCALE * jnp.einsum(
        "tkgd,skd->kgts", query_low, key_low, preferred_element_type=F32
    )
    probs, probs_back = jax.vjp(attention_probs, scores)
    probs_low = probs.astype(BF16)
    attended = jnp.einsum("kgts,skd->tkgd", probs_low, value_low, preferred_element_type=F32)
    attended = attended.reshape(tokens, q_heads * HEAD_DIM).astype(BF16)
    attended_cols = columns_of_all(attended)
    middle = inputs + RESIDUAL * sum_home(product(attended_cols, w_out))
    r2 = rms_scale(middle)
    xn_two = (middle * r2 * gain_two).astype(BF16)

    mask_pad = jnp.pad(mask.astype(BF16), ((0, 0), (0, -experts % 128)))
    x_all, mask_all = gather_expert([xn_two, mask_pad], 1)
    mask_all = mask_all[:, :experts]
    logits_all = jnp.where(mask_all > 0, product(x_all, router_w), NEGATIVE)
    gates_all = jax.nn.softmax(logits_all, axis=-1)
    mine = jnp.arange(experts, dtype=jnp.int32) == lax.axis_index("expert")
    gate = jnp.sum(jnp.where(mine, gates_all, 0.0), axis=-1, keepdims=True)
    gate_up = product(x_all, w_gu)
    g, u = gate_up[:, :ffn], gate_up[:, ffn:]
    sig = jax.nn.sigmoid(g)
    hid = (g * sig * u).astype(BF16)
    y = product(hid, w_dn).astype(BF16).astype(F32)
    og_scaled = RESIDUAL * og_all.astype(F32)
    dy = (gate * og_scaled).astype(BF16)
    gate_grad_col = jnp.sum(y * og_scaled, axis=-1, keepdims=True)
    high = gate_grad_col.astype(BF16)
    low = (gate_grad_col - high.astype(F32)).astype(BF16)
    extra = jnp.concatenate([jnp.where(mine, high, 0), jnp.where(mine, low, 0)], axis=1)
    extra = jnp.pad(extra, ((0, 0), (0, -extra.shape[1] % 128)))
    dy, gated = lax.optimization_barrier((dy, (gate * y).astype(BF16)))
    mixture = lax.psum_scatter(gated, "expert", scatter_dimension=0, tiled=True)
    dhid = right_transposed(dy, w_dn)
    dgu = jnp.concatenate(
        [dhid * u * sig * (1.0 + g * (1.0 - sig)), dhid * g * sig], axis=1
    ).astype(BF16)
    row_grad = right_transposed(dgu, w_gu).astype(BF16)
    down_local, gate_up_local = left_product(hid, dy), left_product(x_all, dgu)
    row_grad, down_local, gate_up_local = lax.optimization_barrier(
        (row_grad, down_local, gate_up_local)
    )
    down_sum, gate_up_sum = sum_pieces(down_local, 1), sum_pieces(gate_up_local, 1)
    scattered = scatter_expert(jnp.concatenate([row_grad, extra], axis=1), 2)
    token_grad = scattered[:, :model_width]
    gate_grad = (
        scattered[:, model_width : model_width + experts]
        + scattered[:, model_width + experts : model_width + 2 * experts]
    )

    upstream = out_grad.astype(F32)
    gates = jax.nn.softmax(
        jnp.where(mask, product(xn_two, router_w), NEGATIVE), axis=-1
    )
    gate_grad = jnp.where(mask, gate_grad, 0.0)
    logit_grad = (
        gates * (gate_grad - jnp.sum(gates * gate_grad, axis=-1, keepdims=True))
    ).astype(BF16)
    xn_two_grad = token_grad + right_transposed(logit_grad, router_w)
    scaled_two = middle * r2
    gain_two_grad = jnp.sum(xn_two_grad * scaled_two, axis=0)
    w2 = xn_two_grad * gain_two
    middle_grad = (
        upstream + r2 * (w2 - scaled_two * jnp.mean(w2 * scaled_two, axis=-1, keepdims=True))
    )
    branch_low = (RESIDUAL * middle_grad).astype(BF16)
    router_local = left_product(xn_two, logit_grad)
    branch_low, down_sum, gate_up_sum = lax.optimization_barrier(
        (branch_low, down_sum, gate_up_sum)
    )
    branch_all = rows_of_all(branch_low)
    attended_grad = columns_home(right_transposed(branch_all, w_out).astype(BF16))
    output_local = left_product(attended_cols, branch_all).astype(BF16)
    small_local = sum_pieces(
        jnp.concatenate([router_local, gain_two_grad[:, None]], axis=1), 0, F32
    )

    attended_grad, mixture = lax.optimization_barrier((attended_grad, mixture))
    attended_grad = attended_grad.reshape(tokens, kv_heads, groups, HEAD_DIM)
    value_grad = jnp.einsum(
        "kgts,tkgd->skd", probs_low, attended_grad, preferred_element_type=F32
    )
    probs_grad = jnp.einsum(
        "tkgd,skd->kgts", attended_grad, value_low, preferred_element_type=F32
    )
    (score_grad,) = probs_back(probs_grad)
    score_low = score_grad.astype(BF16)
    query_grad = SCORE_SCALE * jnp.einsum(
        "kgts,skd->tkgd", score_low, key_low, preferred_element_type=F32
    )
    key_grad = SCORE_SCALE * jnp.einsum(
        "kgts,tkgd->skd", score_low, query_low, preferred_element_type=F32
    )
    (query_raw_grad,) = query_back(query_grad.reshape(tokens, q_heads, HEAD_DIM))
    (key_raw_grad,) = key_back(key_grad)
    qkv_grad = jnp.concatenate(
        [
            query_raw_grad.reshape(tokens, q_width).astype(BF16),
            key_raw_grad.reshape(tokens, kv_width).astype(BF16),
            value_grad.reshape(tokens, kv_width).astype(BF16),
        ],
        axis=1,
    )
    output = (middle + RESIDUAL * mixture.astype(F32)).astype(BF16)
    qkv_all = rows_of_all(qkv_grad)
    xn_one_grad = (
        right_transposed(qkv_all[:, :q_width], w_query)
        + right_transposed(qkv_all[:, q_width : q_width + kv_width], w_key)
        + right_transposed(qkv_all[:, q_width + kv_width :], w_value)
    )
    gain_one_grad = jnp.sum(xn_one_grad * scaled_cols, axis=0)
    small_local = jnp.concatenate([small_local, gain_one_grad[:, None]], axis=1)
    small_pad = jnp.pad(small_local, ((0, 0), (0, -small_local.shape[1] % 128)))
    sums = sum_expert(
        jnp.concatenate(
            [left_product(xn_one, qkv_all).astype(BF16), output_local, small_pad.astype(BF16)],
            axis=1,
        ),
        3,
    ).astype(F32)
    w1 = columns_home((xn_one_grad * gain_one).astype(BF16)).astype(F32)
    scaled_one = inputs * r1
    input_grad = (
        middle_grad + r1 * (w1 - scaled_one * jnp.mean(w1 * scaled_one, axis=-1, keepdims=True))
    ).astype(BF16)

    out_at = q_width + 2 * kv_width
    small_at = out_at + model_width
    return (
        output,
        input_grad,
        sums[:, small_at + experts + 1],
        sums[:, :q_width],
        sums[:, q_width : q_width + kv_width],
        sums[:, q_width + kv_width : out_at],
        sums[:, out_at:small_at],
        sums[:, small_at + experts],
        sums[:, small_at : small_at + experts],
        gate_up_sum[None],
        down_sum[None],
    )


def solution(mesh):
    placed = (
        P(("expert", "shard"), None),
        P("shard"),
        P("shard", None),
        P("shard", None),
        P("shard", None),
        P("shard", None),
        P("shard"),
        P("shard", None),
        P("expert", None, None),
        P("expert", None, None),
        P(("expert", "shard"), None),
        P(("expert", "shard"), None),
    )
    return jax.shard_map(
        shards,
        mesh=mesh,
        in_specs=placed,
        out_specs=(
            P(("expert", "shard"), None),
            P(("expert", "shard"), None),
            P("shard"),
            P("shard", None),
            P("shard", None),
            P("shard", None),
            P("shard", None),
            P("shard"),
            P("shard", None),
            P("expert", None, "shard"),
            P("expert", None, "shard"),
        ),
        check_vma=False,
    )
```
